32 devices in a mesh: row: 4 (over z), col: 4 (over y, core), rep: 2 (over x).
Axes of the slice: x: 2, y: 2, z: 4, core: 2. Of those that a mesh axis runs over, the one named last changes fastest.
Arguments:
- spectra: bfloat16 [2, 8, 64, 2048], P(None, 'row', 'rep', 'col'), parts along dimension 2, may hold values from -60 to 60, as said below
Outputs:
- correlation: bfloat16 [12, 2048, 2048], P('rep', 'row', 'col'), parts along dimension 0
The draws below stay inside these ranges and needn't reach their ends.
There are 2 independent parts, one for each index of `rep`. The reference program is written for one: setup_inputs(seed, part) draws one part's arguments, and reference() takes and returns one part's arrays. A program takes and returns all parts, laid end to end along the dimension named above; each array names one. Nothing has to cross between parts.
Inputs may be any that keep to these rules, and one draw needn't show every extreme that they name: `spectra`: spectral samples.
All inputs are finite; a program needn't handle non-finite values.
Results may differ from the reference program's by a relative error of at most 0.0065.
Values may be sent and summed in bfloat16 or wider, within the bound.
A program may use at most 64 MiB of HBM per device.

```python
import math
import jax
import jax.numpy as jnp
from jax import lax

BINS = 32
LAGS = 6
CHANNELS = 2048
WINDOWS = 8


def draw_spectra(key, part):
    k_base, k_bins, k_chan = jax.random.split(key, 3)
    shape = (2, WINDOWS, BINS, CHANNELS)
    bin_scale = jnp.exp(jax.random.uniform(k_bins, (1, WINDOWS, BINS, CHANNELS), jnp.float32, math.log(0.3), math.log(3.0)))
    chan_scale = jnp.exp(jax.random.uniform(k_chan, (1, WINDOWS, 1, CHANNELS), jnp.float32, math.log(0.2), math.log(5.0)))
    base = jnp.clip(jax.random.normal(k_base, shape, jnp.float32), -4.0, 4.0)
    return (base * bin_scale * chan_scale).astype(jnp.bfloat16)


def setup_inputs(seed: int = 0, part: int = 0) -> dict:
    streams_of = jax.random.split(jax.random.key(seed), 2)
    part_keys = jax.random.split(jax.random.fold_in(streams_of[1], part), 2)
    spectra = draw_spectra(jax.random.fold_in(jax.random.fold_in(streams_of[1], part), 71), part)
    return {"spectra": spectra}


def whiten(spectra):
    values = spectra.astype(jnp.float32)
    power = lax.optimization_barrier(jnp.mean(values * values, axis=(0, 2), keepdims=True))
    return (values / jnp.sqrt(power + 1e-05)).astype(jnp.bfloat16)

def phase_tables(bins, lags):
    freq = jnp.arange(bins).astype(jnp.float32) + 1.0
    shift = 2.0 * jnp.arange(lags).astype(jnp.float32) - lags + 1.0
    angle = math.pi * shift[:, None] * freq[None, :] / bins
    return (jnp.cos(angle), jnp.sin(angle))

def reference(spectra):
    white = whiten(spectra)
    cosine, sine = phase_tables(BINS, LAGS)
    flat = white.reshape(2 * WINDOWS * BINS, CHANNELS)
    values = white.astype(jnp.float32)
    scale = 1.0 / math.sqrt(WINDOWS * BINS)

    def one_lag(tables):
        cos_row, sin_row = tables
        c_term = cos_row[None, :, None]
        s_term = sin_row[None, :, None]
        real_part = values[0] * c_term - values[1] * s_term
        imag_part = values[0] * s_term + values[1] * c_term
        turned = jnp.stack([real_part, imag_part]).astype(jnp.bfloat16).reshape(2 * WINDOWS * BINS, CHANNELS)
        summed = jnp.dot(flat.T, turned, preferred_element_type=jnp.float32)
        return (summed * scale).astype(jnp.bfloat16)
    return lax.map(one_lag, (cosine, sine))
```

```python
import functools
import math

import jax
import jax.numpy as jnp
import numpy as np
from jax import lax
from jax.experimental import pallas as pl
from jax.experimental.pallas import tpu as pltpu
from jax.sharding import PartitionSpec as P

LAGS = 6
MESH = pl.DeviceIdType.MESH
LEFT, RIGHT = 0, 1


def phase_table(bins, lags):
    freq = np.arange(bins, dtype=np.float32) + np.float32(1.0)
    shift = np.float32(2.0) * np.arange(lags, dtype=np.float32) - np.float32(lags - 1.0)
    angle = (np.float32(math.pi) * shift[None, :] * freq[:, None] / np.float32(bins)).astype(np.float32)
    return np.concatenate([np.cos(angle), np.sin(angle)], axis=1).astype(np.float32)


def kernel(n, m, scale, x_hbm, tab_hbm, out_ref, x, tab, col, row, row_t, turned,
           in_sem, z_send, z_recv, c_send, f_send, r_recv):
    _, wl, bins, cl = x.shape
    half = wl * bins
    depth = 2 * half
    q = m // n
    chips = m // 2
    r = lax.axis_index("row")
    c = lax.axis_index("col")
    chip = c // 2
    core = c % 2
    sib = chip * 2 + (1 - core)

    load_x = pltpu.make_async_copy(x_hbm, x, in_sem.at[0])
    load_t = pltpu.make_async_copy(tab_hbm, tab, in_sem.at[1])
    load_x.start()
    load_t.start()

    barrier = pltpu.get_barrier_semaphore()
    for d in range(1, m):
        pl.semaphore_signal(barrier, inc=1, device_id={"col": (c + d) % m}, device_id_type=MESH)

    @pl.when(r > 0)
    def _():
        pl.semaphore_signal(barrier, inc=1, device_id={"row": r - 1}, device_id_type=MESH)

    @pl.when(r < n - 1)
    def _():
        pl.semaphore_signal(barrier, inc=1, device_id={"row": r + 1}, device_id_type=MESH)

    load_x.wait()
    for w in range(wl):
        re = x[0, w].astype(jnp.float32)
        im = x[1, w].astype(jnp.float32)
        power = jnp.sum(re * re + im * im, axis=0, keepdims=True) / (2.0 * bins)
        root = jnp.sqrt(power + 1e-05)
        col[r, 0, w * bins:(w + 1) * bins, :] = (re / root).astype(jnp.bfloat16)
        col[r, 1, w * bins:(w + 1) * bins, :] = (im / root).astype(jnp.bfloat16)

    pl.semaphore_wait(barrier, (m - 1) + (r > 0).astype(jnp.int32) + (r < n - 1).astype(jnp.int32))

    def z_copy(way, s, part):
        src = r - s if way == RIGHT else r + s
        to = r + 1 if way == RIGHT else r - 1
        return pltpu.make_async_remote_copy(
            src_ref=col.at[src, part], dst_ref=col.at[src, part],
            send_sem=z_send.at[way, s, part], recv_sem=z_recv.at[way, s, part],
            device_id={"row": to}, device_id_type=MESH)

    def z_sends(way, s):
        if way == RIGHT:
            return jnp.logical_and(r - s >= 0, r + 1 < n)
        return jnp.logical_and(r + s < n, r - 1 >= 0)

    def z_got(way, s):
        if way == RIGHT:
            return r - 1 - s >= 0
        return r + 1 + s < n

    def z_src(way, s):
        return r - 1 - s if way == RIGHT else r + 1 + s

    def slot_of(way, s):
        return 1 + 2 * s + way

    def owns(o):
        return c == r * q + o

    def own_copies(o, src, slot, part):
        copies = []
        for p in range(1, chips):
            copies.append(pltpu.make_async_remote_copy(
                src_ref=col.at[src, part], dst_ref=row.at[o, src, part],
                send_sem=c_send.at[slot, part, p], recv_sem=r_recv.at[o, slot, part],
                device_id={"col": ((chip + p) % chips) * 2 + part}, device_id_type=MESH))
        copies.append(pltpu.make_async_remote_copy(
            src_ref=col.at[src, part], dst_ref=row.at[o, src, part],
            send_sem=c_send.at[slot, part, 0], recv_sem=r_recv.at[o, slot, part],
            device_id={"col": sib}, device_id_type=MESH))
        return copies

    def swap_copy(o, src, slot, part):
        return pltpu.make_async_remote_copy(
            src_ref=row.at[o, src, part], dst_ref=row.at[o, src, part],
            send_sem=f_send.at[o, slot], recv_sem=r_recv.at[o, slot, part],
            device_id={"col": sib}, device_id_type=MESH)

    def hand_out(src, slot, part):
        for o in range(q):
            @pl.when(owns(o))
            def _():
                for copy in own_copies(o, src, slot, part):
                    copy.start()

    def far(o):
        return chip != (r * q + o) // 2

    def swap(src, slot):
        for o in range(q):
            for part in range(2):
                @pl.when(jnp.logical_and(far(o), core == part))
                def _():
                    swap_copy(o, src, slot, part).wait_recv()
                    swap_copy(o, src, slot, part).start()

    def turn(src):
        base = pl.multiple_of(src * depth, depth)
        for w in range(wl):
            rows = slice(w * bins, (w + 1) * bins)
            re = col[src, 0, rows, :].astype(jnp.float32)
            im = col[src, 1, rows, :].astype(jnp.float32)
            for t in range(LAGS):
                cos = tab[:, t:t + 1]
                sin = tab[:, LAGS + t:LAGS + t + 1]
                turned[t, pl.ds(base + w * bins, bins), :] = (re * cos - im * sin).astype(jnp.bfloat16)
                turned[t, pl.ds(base + half + w * bins, bins), :] = (re * sin + im * cos).astype(jnp.bfloat16)

    def flip(src, slot):
        base = pl.multiple_of(src * depth, depth)
        for o in range(q):
            chans = slice(o * cl, (o + 1) * cl)

            @pl.when(owns(o))
            def _():
                row_t[chans, pl.ds(base, depth)] = col[src].reshape(depth, cl).T

            @pl.when(jnp.logical_not(owns(o)))
            def _():
                for part in range(2):
                    @pl.when(jnp.logical_or(jnp.logical_not(far(o)), core != part))
                    def _():
                        swap_copy(o, src, slot, part).wait_recv()
                row_t[chans, pl.ds(base, depth)] = row[o, src].reshape(depth, cl).T

    for part in range(2):
        for way in (LEFT, RIGHT):
            @pl.when(z_sends(way, 0))
            def _():
                z_copy(way, 0, part).start()
        hand_out(r, 0, part)
    load_t.wait()
    turn(r)

    def each(s, fn):
        if s < 0:
            fn(r, 0)
            return
        for way in (LEFT, RIGHT):
            @pl.when(z_got(way, s))
            def _():
                fn(z_src(way, s), slot_of(way, s))

    for s in range(n - 1):
        for part in range(2):
            for way in (LEFT, RIGHT):
                @pl.when(z_got(way, s))
                def _():
                    z_copy(way, s, part).wait_recv()
                    if s + 1 < n - 1:
                        @pl.when(z_sends(way, s + 1))
                        def _():
                            z_copy(way, s + 1, part).start()
                    hand_out(z_src(way, s), slot_of(way, s), part)
        each(s - 1, swap)
        each(s, lambda src, slot: turn(src))
        each(s - 1, flip)
    each(n - 2, swap)
    each(n - 2, flip)

    for t in range(LAGS):
        total = jnp.dot(row_t[...], turned[t], preferred_element_type=jnp.float32)
        out_ref[t] = (total * scale).astype(out_ref.dtype)

    for s in range(n - 1):
        for way in (LEFT, RIGHT):
            @pl.when(z_sends(way, s))
            def _():
                for part in range(2):
                    z_copy(way, s, part).wait_send()

    def drain(src, slot):
        for o in range(q):
            @pl.when(owns(o))
            def _():
                for part in range(2):
                    for copy in own_copies(o, src, slot, part):
                        copy.wait_send()
            for part in range(2):
                @pl.when(jnp.logical_and(far(o), core == part))
                def _():
                    swap_copy(o, src, slot, part).wait_send()

    for s in range(-1, n - 1):
        each(s, drain)


def correlate(n, m, spectra):
    _, wl, bins, cl = spectra.shape
    q = m // n
    half = wl * bins
    depth = 2 * half
    slots = 2 * n - 1
    scale = 1.0 / math.sqrt(n * wl * bins)
    table = jnp.asarray(phase_table(bins, LAGS))
    sizes = (n * depth * cl * (1 + 2 * q + LAGS) + LAGS * q * cl * cl) * 2
    dma = pltpu.SemaphoreType.DMA
    return pl.pallas_call(
        functools.partial(kernel, n, m, scale),
        out_shape=pltpu.VMEM((LAGS, q * cl, cl), jnp.bfloat16),
        in_specs=[pl.BlockSpec(memory_space=pltpu.HBM)] * 2,
        out_specs=pl.BlockSpec(memory_space=pltpu.VMEM),
        scratch_shapes=[
            pltpu.VMEM(spectra.shape, jnp.bfloat16),
            pltpu.VMEM(table.shape, jnp.float32),
            pltpu.VMEM((n, 2, half, cl), jnp.bfloat16),
            pltpu.VMEM((q, n, 2, half, cl), jnp.bfloat16),
            pltpu.VMEM((q * cl, n * depth), jnp.bfloat16),
            pltpu.VMEM((LAGS, n * depth, cl), jnp.bfloat16),
            dma((2,)),
            dma((2, n - 1, 2)),
            dma((2, n - 1, 2)),
            dma((slots, 2, m // 2)),
            dma((q, slots)),
            dma((q, slots, 2)),
        ],
        compiler_params=pltpu.CompilerParams(
            collective_id=0, has_side_effects=True, vmem_limit_bytes=sizes + (16 << 20)),
        cost_estimate=pl.CostEstimate(
            flops=2 * LAGS * n * depth * q * cl * cl,
            bytes_accessed=LAGS * q * cl * cl * 2, transcendentals=0),
    )(spectra, table)


def solution(mesh):
    n, m = mesh.shape["row"], mesh.shape["col"]
    return jax.shard_map(
        functools.partial(correlate, n, m), mesh=mesh,
        in_specs=(P(None, "row", "rep", "col"),), out_specs=P("rep", "row", "col"), check_vma=False)
```

```python
import functools
import math

import jax
import jax.numpy as jnp
import numpy as np
from jax import lax
from jax.experimental import pallas as pl
from jax.experimental.pallas import tpu as pltpu
from jax.sharding import PartitionSpec as P

LAGS = 6
MESH = pl.DeviceIdType.MESH
LEFT, RIGHT = 0, 1


def phase_table(bins, lags):
    freq = np.arange(bins, dtype=np.float32) + np.float32(1.0)
    shift = np.float32(2.0) * np.arange(lags, dtype=np.float32) - np.float32(lags - 1.0)
    angle = (np.float32(math.pi) * shift[None, :] * freq[:, None] / np.float32(bins)).astype(np.float32)
    return np.concatenate([np.cos(angle), np.sin(angle)], axis=1).astype(np.float32)


def gather(n, m, x_hbm, tab_hbm, row_t, turned, x, tab, col, row,
           in_sem, z_send, z_recv, c_send, f_send, r_recv):
    _, wl, bins, cl = x.shape
    half = wl * bins
    depth = 2 * half
    q = m // n
    chips = m // 2
    r = lax.axis_index("row")
    c = lax.axis_index("col")
    chip = c // 2
    core = c % 2
    sib = chip * 2 + (1 - core)

    load_x = pltpu.make_async_copy(x_hbm, x, in_sem.at[0])
    load_t = pltpu.make_async_copy(tab_hbm, tab, in_sem.at[1])
    load_x.start()
    load_t.start()

    barrier = pltpu.get_barrier_semaphore()
    for d in range(1, m):
        pl.semaphore_signal(barrier, inc=1, device_id={"col": (c + d) % m}, device_id_type=MESH)

    @pl.when(r > 0)
    def _():
        pl.semaphore_signal(barrier, inc=1, device_id={"row": r - 1}, device_id_type=MESH)

    @pl.when(r < n - 1)
    def _():
        pl.semaphore_signal(barrier, inc=1, device_id={"row": r + 1}, device_id_type=MESH)

    load_x.wait()
    for w in range(wl):
        re = x[0, w].astype(jnp.float32)
        im = x[1, w].astype(jnp.float32)
        power = jnp.sum(re * re + im * im, axis=0, keepdims=True) / (2.0 * bins)
        root = jnp.sqrt(power + 1e-05)
        col[r, 0, w * bins:(w + 1) * bins, :] = (re / root).astype(jnp.bfloat16)
        col[r, 1, w * bins:(w + 1) * bins, :] = (im / root).astype(jnp.bfloat16)

    pl.semaphore_wait(barrier, (m - 1) + (r > 0).astype(jnp.int32) + (r < n - 1).astype(jnp.int32))

    def z_copy(way, s, part):
        src = r - s if way == RIGHT else r + s
        to = r + 1 if way == RIGHT else r - 1
        return pltpu.make_async_remote_copy(
            src_ref=col.at[src, part], dst_ref=col.at[src, part],
            send_sem=z_send.at[way, s, part], recv_sem=z_recv.at[way, s, part],
            device_id={"row": to}, device_id_type=MESH)

    def z_sends(way, s):
        if way == RIGHT:
            return jnp.logical_and(r - s >= 0, r + 1 < n)
        return jnp.logical_and(r + s < n, r - 1 >= 0)

    def z_got(way, s):
        if way == RIGHT:
            return r - 1 - s >= 0
        return r + 1 + s < n

    def z_src(way, s):
        return r - 1 - s if way == RIGHT else r + 1 + s

    def slot_of(way, s):
        return 1 + 2 * s + way

    def owns(o):
        return c == r * q + o

    def own_copies(o, src, slot, part):
        copies = []
        for p in range(1, chips):
            copies.append(pltpu.make_async_remote_copy(
                src_ref=col.at[src, part], dst_ref=row.at[o, src, part],
                send_sem=c_send.at[slot, part, p], recv_sem=r_recv.at[o, slot, part],
                device_id={"col": ((chip + p) % chips) * 2 + part}, device_id_type=MESH))
        copies.append(pltpu.make_async_remote_copy(
            src_ref=col.at[src, part], dst_ref=row.at[o, src, part],
            send_sem=c_send.at[slot, part, 0], recv_sem=r_recv.at[o, slot, part],
            device_id={"col": sib}, device_id_type=MESH))
        return copies

    def swap_copy(o, src, slot, part):
        return pltpu.make_async_remote_copy(
            src_ref=row.at[o, src, part], dst_ref=row.at[o, src, part],
            send_sem=f_send.at[o, slot], recv_sem=r_recv.at[o, slot, part],
            device_id={"col": sib}, device_id_type=MESH)

    def hand_out(src, slot, part):
        for o in range(q):
            @pl.when(owns(o))
            def _():
                for copy in own_copies(o, src, slot, part):
                    copy.start()

    def far(o):
        return chip != (r * q + o) // 2

    def swap(src, slot):
        for o in range(q):
            for part in range(2):
                @pl.when(jnp.logical_and(far(o), core == part))
                def _():
                    swap_copy(o, src, slot, part).wait_recv()
                    swap_copy(o, src, slot, part).start()

    def turn(src):
        base = pl.multiple_of(src * depth, depth)
        for w in range(wl):
            rows = slice(w * bins, (w + 1) * bins)
            re = col[src, 0, rows, :].astype(jnp.float32)
            im = col[src, 1, rows, :].astype(jnp.float32)
            for t in range(LAGS):
                cos = tab[:, t:t + 1]
                sin = tab[:, LAGS + t:LAGS + t + 1]
                turned[t, pl.ds(base + w * bins, bins), :] = (re * cos - im * sin).astype(jnp.bfloat16)
                turned[t, pl.ds(base + half + w * bins, bins), :] = (re * sin + im * cos).astype(jnp.bfloat16)

    def flip(src, slot):
        base = pl.multiple_of(src * depth, depth)
        for o in range(q):
            chans = slice(o * cl, (o + 1) * cl)

            @pl.when(owns(o))
            def _():
                row_t[chans, pl.ds(base, depth)] = col[src].reshape(depth, cl).T

            @pl.when(jnp.logical_not(owns(o)))
            def _():
                for part in range(2):
                    @pl.when(jnp.logical_or(jnp.logical_not(far(o)), core != part))
                    def _():
                        swap_copy(o, src, slot, part).wait_recv()
                row_t[chans, pl.ds(base, depth)] = row[o, src].reshape(depth, cl).T

    for part in range(2):
        for way in (LEFT, RIGHT):
            @pl.when(z_sends(way, 0))
            def _():
                z_copy(way, 0, part).start()
        hand_out(r, 0, part)
    load_t.wait()
    turn(r)

    def each(s, fn):
        if s < 0:
            fn(r, 0)
            return
        for way in (LEFT, RIGHT):
            @pl.when(z_got(way, s))
            def _():
                fn(z_src(way, s), slot_of(way, s))

    for s in range(n - 1):
        for part in range(2):
            for way in (LEFT, RIGHT):
                @pl.when(z_got(way, s))
                def _():
                    z_copy(way, s, part).wait_recv()
                    if s + 1 < n - 1:
                        @pl.when(z_sends(way, s + 1))
                        def _():
                            z_copy(way, s + 1, part).start()
                    hand_out(z_src(way, s), slot_of(way, s), part)
        each(s - 1, swap)
        each(s, lambda src, slot: turn(src))
        each(s - 1, flip)
    each(n - 2, swap)
    each(n - 2, flip)

    for s in range(n - 1):
        for way in (LEFT, RIGHT):
            @pl.when(z_sends(way, s))
            def _():
                for part in range(2):
                    z_copy(way, s, part).wait_send()

    def drain(src, slot):
        for o in range(q):
            @pl.when(owns(o))
            def _():
                for part in range(2):
                    for copy in own_copies(o, src, slot, part):
                        copy.wait_send()
            for part in range(2):
                @pl.when(jnp.logical_and(far(o), core == part))
                def _():
                    swap_copy(o, src, slot, part).wait_send()

    for s in range(-1, n - 1):
        each(s, drain)


def multiply(scale, row_t, turned, out_hbm, out, sem):
    copies = []
    for t in range(LAGS):
        total = jnp.dot(row_t[...], turned[t], preferred_element_type=jnp.float32)
        out[t] = (total * scale).astype(out.dtype)
        copies.append(pltpu.make_async_copy(out.at[t], out_hbm.at[t], sem.at[t]))
        copies[t].start()
    for copy in copies:
        copy.wait()


def correlate(n, m, spectra):
    _, wl, bins, cl = spectra.shape
    q = m // n
    half = wl * bins
    depth = 2 * half
    slots = 2 * n - 1
    scale = 1.0 / math.sqrt(n * wl * bins)
    spectra = pltpu.with_memory_space_constraint(spectra, pltpu.HBM)
    table = pltpu.with_memory_space_constraint(jnp.asarray(phase_table(bins, LAGS)), pltpu.HBM)
    dma = pltpu.SemaphoreType.DMA
    vmem = pl.BlockSpec(memory_space=pltpu.VMEM)
    hbm = pl.BlockSpec(memory_space=pltpu.HBM)
    row_t, turned = pl.pallas_call(
        functools.partial(gather, n, m),
        out_shape=(pltpu.VMEM((q * cl, n * depth), jnp.bfloat16),
                   pltpu.VMEM((LAGS, n * depth, cl), jnp.bfloat16)),
        in_specs=[hbm, hbm],
        out_specs=(vmem, vmem),
        scratch_shapes=[
            pltpu.VMEM(spectra.shape, jnp.bfloat16),
            pltpu.VMEM(table.shape, jnp.float32),
            pltpu.VMEM((n, 2, half, cl), jnp.bfloat16),
            pltpu.VMEM((q, n, 2, half, cl), jnp.bfloat16),
            dma((2,)),
            dma((2, n - 1, 2)),
            dma((2, n - 1, 2)),
            dma((slots, 2, m // 2)),
            dma((q, slots)),
            dma((q, slots, 2)),
        ],
        compiler_params=pltpu.CompilerParams(
            collective_id=0, has_side_effects=True,
            vmem_limit_bytes=2 * n * depth * cl * (2 + q) + (8 << 20)),
        name="gather",
    )(spectra, table)
    row_t = pltpu.with_memory_space_constraint(row_t, pltpu.VMEM)
    turned = pltpu.with_memory_space_constraint(turned, pltpu.VMEM)
    return pl.pallas_call(
        functools.partial(multiply, scale),
        out_shape=jax.ShapeDtypeStruct((LAGS, q * cl, cl), jnp.bfloat16),
        in_specs=[vmem, vmem],
        out_specs=hbm,
        scratch_shapes=[pltpu.VMEM((LAGS, q * cl, cl), jnp.bfloat16), dma((LAGS,))],
        compiler_params=pltpu.CompilerParams(vmem_limit_bytes=2 * LAGS * q * cl * cl + (16 << 20)),
        name="multiply",
    )(row_t, turned)


def solution(mesh):
    n, m = mesh.shape["row"], mesh.shape["col"]
    return jax.shard_map(
        functools.partial(correlate, n, m), mesh=mesh,
        in_specs=(P(None, "row", "rep", "col"),), out_specs=P("rep", "row", "col"), check_vma=False)
```

```python
import functools
import math

import jax
import jax.numpy as jnp
import numpy as np
from jax import lax
from jax.experimental import pallas as pl
from jax.experimental.pallas import tpu as pltpu
from jax.sharding import PartitionSpec as P

LAGS = 6
MESH = pl.DeviceIdType.MESH
LEFT, RIGHT = 0, 1


def phase_table(bins, lags):
    freq = np.arange(bins, dtype=np.float32) + np.float32(1.0)
    shift = np.float32(2.0) * np.arange(lags, dtype=np.float32) - np.float32(lags - 1.0)
    angle = (np.float32(math.pi) * shift[None, :] * freq[:, None] / np.float32(bins)).astype(np.float32)
    return np.concatenate([np.cos(angle), np.sin(angle)], axis=1).astype(np.float32)


def gather(n, m, x_hbm, tab_hbm, row_t, turned, x, tab, col, row,
           in_sem, z_send, z_recv, c_send, f_send, r_recv):
    _, wl, bins, cl = x.shape
    half = wl * bins
    depth = 2 * half
    q = m // n
    chips = m // 2
    r = lax.axis_index("row")
    c = lax.axis_index("col")
    chip = c // 2
    core = c % 2
    sib = chip * 2 + (1 - core)

    load_x = pltpu.make_async_copy(x_hbm, x, in_sem.at[0])
    load_t = pltpu.make_async_copy(tab_hbm, tab, in_sem.at[1])
    load_x.start()
    load_t.start()

    barrier = pltpu.get_barrier_semaphore()
    for d in range(1, m):
        pl.semaphore_signal(barrier, inc=1, device_id={"col": (c + d) % m}, device_id_type=MESH)

    for step in (1, n - 1):
        pl.semaphore_signal(barrier, inc=1, device_id={"row": (r + step) % n}, device_id_type=MESH)

    load_x.wait()
    for w in range(wl):
        re = x[0, w].astype(jnp.float32)
        im = x[1, w].astype(jnp.float32)
        power = jnp.sum(re * re + im * im, axis=0, keepdims=True) / (2.0 * bins)
        root = jnp.sqrt(power + 1e-05)
        col[r, 0, w * bins:(w + 1) * bins, :] = (re / root).astype(jnp.bfloat16)
        col[r, 1, w * bins:(w + 1) * bins, :] = (im / root).astype(jnp.bfloat16)

    pl.semaphore_wait(barrier, m + 1)

    last = n - 2

    def straight(s):
        return s == last and n > 2

    def z_copy(way, s, part):
        if straight(s):
            src = r
            to = n - 1 if way == RIGHT else 0
        else:
            src = r - s if way == RIGHT else r + s
            to = r + 1 if way == RIGHT else r - 1
        return pltpu.make_async_remote_copy(
            src_ref=col.at[src, part], dst_ref=col.at[src, part],
            send_sem=z_send.at[way, s, part], recv_sem=z_recv.at[way, s, part],
            device_id={"row": to}, device_id_type=MESH)

    def z_sends(way, s):
        if straight(s):
            return r == (0 if way == RIGHT else n - 1)
        if way == RIGHT:
            return jnp.logical_and(r - s >= 0, r + 1 < n)
        return jnp.logical_and(r + s < n, r - 1 >= 0)

    def z_got(way, s):
        if way == RIGHT:
            return r - 1 - s >= 0
        return r + 1 + s < n

    def z_src(way, s):
        return r - 1 - s if way == RIGHT else r + 1 + s

    def slot_of(way, s):
        return 1 + 2 * s + way

    def owns(o):
        return c == r * q + o

    def own_copies(o, src, slot, part):
        copies = []
        for p in range(1, chips):
            copies.append(pltpu.make_async_remote_copy(
                src_ref=col.at[src, part], dst_ref=row.at[o, src, part],
                send_sem=c_send.at[slot, part, p], recv_sem=r_recv.at[o, slot, part],
                device_id={"col": ((chip + p) % chips) * 2 + part}, device_id_type=MESH))
        copies.append(pltpu.make_async_remote_copy(
            src_ref=col.at[src, part], dst_ref=row.at[o, src, part],
            send_sem=c_send.at[slot, part, 0], recv_sem=r_recv.at[o, slot, part],
            device_id={"col": sib}, device_id_type=MESH))
        return copies

    def swap_copy(o, src, slot, part):
        return pltpu.make_async_remote_copy(
            src_ref=row.at[o, src, part], dst_ref=row.at[o, src, part],
            send_sem=f_send.at[o, slot], recv_sem=r_recv.at[o, slot, part],
            device_id={"col": sib}, device_id_type=MESH)

    def hand_out(src, slot, part):
        for o in range(q):
            @pl.when(owns(o))
            def _():
                for copy in own_copies(o, src, slot, part):
                    copy.start()

    def far(o):
        return chip != (r * q + o) // 2

    def swap(src, slot):
        for o in range(q):
            for part in range(2):
                @pl.when(jnp.logical_and(far(o), core == part))
                def _():
                    swap_copy(o, src, slot, part).wait_recv()
                    swap_copy(o, src, slot, part).start()

    def turn(src):
        base = pl.multiple_of(src * depth, depth)
        for w in range(wl):
            rows = slice(w * bins, (w + 1) * bins)
            re = col[src, 0, rows, :].astype(jnp.float32)
            im = col[src, 1, rows, :].astype(jnp.float32)
            for t in range(LAGS):
                cos = tab[:, t:t + 1]
                sin = tab[:, LAGS + t:LAGS + t + 1]
                turned[t, pl.ds(base + w * bins, bins), :] = (re * cos - im * sin).astype(jnp.bfloat16)
                turned[t, pl.ds(base + half + w * bins, bins), :] = (re * sin + im * cos).astype(jnp.bfloat16)

    def flip(src, slot):
        base = pl.multiple_of(src * depth, depth)
        for o in range(q):
            chans = slice(o * cl, (o + 1) * cl)

            @pl.when(owns(o))
            def _():
                row_t[chans, pl.ds(base, depth)] = col[src].reshape(depth, cl).T

            @pl.when(jnp.logical_not(owns(o)))
            def _():
                for part in range(2):
                    @pl.when(jnp.logical_or(jnp.logical_not(far(o)), core != part))
                    def _():
                        swap_copy(o, src, slot, part).wait_recv()
                row_t[chans, pl.ds(base, depth)] = row[o, src].reshape(depth, cl).T

    for way in (LEFT, RIGHT):
        if straight(last):
            @pl.when(z_sends(way, last))
            def _():
                for part in range(2):
                    z_copy(way, last, part).start()
    for part in range(2):
        for way in (LEFT, RIGHT):
            @pl.when(z_sends(way, 0))
            def _():
                z_copy(way, 0, part).start()
        hand_out(r, 0, part)
    load_t.wait()
    turn(r)

    def each(s, fn):
        if s < 0:
            fn(r, 0)
            return
        for way in (LEFT, RIGHT):
            @pl.when(z_got(way, s))
            def _():
                fn(z_src(way, s), slot_of(way, s))

    for s in range(n - 1):
        for part in range(2):
            for way in (LEFT, RIGHT):
                @pl.when(z_got(way, s))
                def _():
                    z_copy(way, s, part).wait_recv()
                    if s + 1 <= last and not straight(s + 1):
                        @pl.when(z_sends(way, s + 1))
                        def _():
                            z_copy(way, s + 1, part).start()
                    hand_out(z_src(way, s), slot_of(way, s), part)
        each(s - 1, swap)
        each(s, lambda src, slot: turn(src))
        each(s - 1, flip)
    each(n - 2, swap)
    each(n - 2, flip)

    for s in range(n - 1):
        for way in (LEFT, RIGHT):
            @pl.when(z_sends(way, s))
            def _():
                for part in range(2):
                    z_copy(way, s, part).wait_send()

    def drain(src, slot):
        for o in range(q):
            @pl.when(owns(o))
            def _():
                for part in range(2):
                    for copy in own_copies(o, src, slot, part):
                        copy.wait_send()
            for part in range(2):
                @pl.when(jnp.logical_and(far(o), core == part))
                def _():
                    swap_copy(o, src, slot, part).wait_send()

    for s in range(-1, n - 1):
        each(s, drain)


def multiply(scale, row_t, turned, out_hbm, out, sem):
    copies = []
    for t in range(LAGS):
        total = jnp.dot(row_t[...], turned[t], preferred_element_type=jnp.float32)
        out[t] = (total * scale).astype(out.dtype)
        copies.append(pltpu.make_async_copy(out.at[t], out_hbm.at[t], sem.at[t]))
        copies[t].start()
    for copy in copies:
        copy.wait()


def correlate(n, m, spectra):
    _, wl, bins, cl = spectra.shape
    q = m // n
    half = wl * bins
    depth = 2 * half
    slots = 2 * n - 1
    scale = 1.0 / math.sqrt(n * wl * bins)
    spectra = pltpu.with_memory_space_constraint(spectra, pltpu.HBM)
    table = pltpu.with_memory_space_constraint(jnp.asarray(phase_table(bins, LAGS)), pltpu.HBM)
    dma = pltpu.SemaphoreType.DMA
    vmem = pl.BlockSpec(memory_space=pltpu.VMEM)
    hbm = pl.BlockSpec(memory_space=pltpu.HBM)
    row_t, turned = pl.pallas_call(
        functools.partial(gather, n, m),
        out_shape=(pltpu.VMEM((q * cl, n * depth), jnp.bfloat16),
                   pltpu.VMEM((LAGS, n * depth, cl), jnp.bfloat16)),
        in_specs=[hbm, hbm],
        out_specs=(vmem, vmem),
        scratch_shapes=[
            pltpu.VMEM(spectra.shape, jnp.bfloat16),
            pltpu.VMEM(table.shape, jnp.float32),
            pltpu.VMEM((n, 2, half, cl), jnp.bfloat16),
            pltpu.VMEM((q, n, 2, half, cl), jnp.bfloat16),
            dma((2,)),
            dma((2, n - 1, 2)),
            dma((2, n - 1, 2)),
            dma((slots, 2, m // 2)),
            dma((q, slots)),
            dma((q, slots, 2)),
        ],
        compiler_params=pltpu.CompilerParams(
            collective_id=0, has_side_effects=True,
            vmem_limit_bytes=2 * n * depth * cl * (2 + q) + (8 << 20)),
        name="gather",
    )(spectra, table)
    row_t = pltpu.with_memory_space_constraint(row_t, pltpu.VMEM)
    turned = pltpu.with_memory_space_constraint(turned, pltpu.VMEM)
    return pl.pallas_call(
        functools.partial(multiply, scale),
        out_shape=jax.ShapeDtypeStruct((LAGS, q * cl, cl), jnp.bfloat16),
        in_specs=[vmem, vmem],
        out_specs=hbm,
        scratch_shapes=[pltpu.VMEM((LAGS, q * cl, cl), jnp.bfloat16), dma((LAGS,))],
        compiler_params=pltpu.CompilerParams(vmem_limit_bytes=2 * LAGS * q * cl * cl + (16 << 20)),
        name="multiply",
    )(row_t, turned)


def solution(mesh):
    n, m = mesh.shape["row"], mesh.shape["col"]
    return jax.shard_map(
        functools.partial(correlate, n, m), mesh=mesh,
        in_specs=(P(None, "row", "rep", "col"),), out_specs=P("rep", "row", "col"), check_vma=False)
```
